256 devices in a mesh: base: 32 (over z_lo, x, core), band: 8 (over z_hi, y).
Axes of the slice: x: 4, y: 4, z: 8 (z_hi: 2, z_lo: 4; z = z_hi * 4 + z_lo), core: 2. Of those that a mesh axis runs over, the one named last changes fastest.
Arguments:
- coherency: float32 [16, 16, 8, 8192], P('band', None, None, 'base'), may hold values from -1.5 to 1.5
- observed: float32 [16, 8, 8192], P('band', None, 'base'), may hold values from -6 to 6
- jones_deviation: float32 [16, 16, 8, 512], P('band', None, None, 'base'), may hold values from -1.8 to 1.8
- antenna_first: int32 [8192], P('base'), may hold values from 0 to 511, as said below
- antenna_second: int32 [8192], P('base'), may hold values from 0 to 511, as said below
Outputs:
- jones: float32 [16, 16, 8, 512], P('band', None, None, 'base')
- residual: float32 [16, 8, 8192], P('band', None, 'base')
The draws below stay inside these ranges and needn't reach their ends.
Inputs may be any that keep to these rules, and one draw needn't show every extreme that they name: `antenna_first`: every station is the first station of exactly 16 baselines. On every baseline antenna_second differs from antenna_first.
All inputs are finite; a program needn't handle non-finite values.
Results may differ from the reference program's by a relative error of at most 0.0003.
Values sent between devices are 32-bit elements; how exact they have to be, the bound alone decides.
No kernel may reach another device: no remote copies, remote signals or barrier semaphores. Data moves between devices by JAX's collectives and lax.ppermute only.
A program may use at most 64 MiB of HBM per device.

```python
import jax
import jax.numpy as jnp
from jax import lax

STATION_TOTAL = 512
DIRECTION_COUNT = 16
SUBBAND_COUNT = 16
ITERS = 3
BASELINE_TOTAL = 8192


def station_pairs(key):
    base_key = jax.random.fold_in(key, 11)
    leading_key = jax.random.fold_in(base_key, 1)
    iteration_key = jax.random.fold_in(base_key, 2)
    first_station = jax.random.permutation(leading_key, jnp.arange(BASELINE_TOTAL, dtype=jnp.int32) % STATION_TOTAL)
    deviation_values = jax.random.randint(iteration_key, (BASELINE_TOTAL,), 1, STATION_TOTAL, dtype=jnp.int32)
    second = (first_station + deviation_values) % STATION_TOTAL
    return (first_station.astype(jnp.int32), second.astype(jnp.int32))


def draw_antenna_first(key, part):
    return station_pairs(key)[0]


def draw_antenna_second(key, part):
    return station_pairs(key)[1]


def shard_levels(rng, dims, shards, least, largest):
    loudness = 1.0
    for axis_at, parts in shards:
        heights = jax.random.uniform(jax.random.fold_in(jax.random.fold_in(rng, 6), axis_at), (parts,), jnp.float32, least / len(shards), largest / len(shards))
        loudness = loudness * jnp.repeat(jnp.exp(heights), dims[axis_at] // parts).reshape((-1,) + (1,) * (len(dims) - 1 - axis_at))
    return loudness


def centred(own_key, shape, deviation, limit, cuts=(), kind=jnp.bfloat16):
    result = deviation * jax.random.normal(own_key, shape, jnp.float32)
    if cuts:
        result = result * shard_levels(own_key, shape, cuts, -0.22, 0.18)
    return jnp.clip(result, -limit, limit).astype(kind)


def setup_inputs(seed: int = 0) -> dict:
    key_list = jax.random.split(jax.random.key(seed), 6)
    return {
        "coherency": centred(key_list[0], (SUBBAND_COUNT, DIRECTION_COUNT, 8, BASELINE_TOTAL), 0.25, 1.5, ((0, 8), (3, 32)), jnp.float32),
        "observed": centred(key_list[1], (SUBBAND_COUNT, 8, BASELINE_TOTAL), 1.0, 6.0, ((0, 8), (2, 32)), jnp.float32),
        "jones_deviation": centred(key_list[2], (SUBBAND_COUNT, DIRECTION_COUNT, 8, STATION_TOTAL), 0.3, 1.8, ((0, 8), (3, 32)), jnp.float32),
        "antenna_first": draw_antenna_first(jax.random.fold_in(key_list[5], 71), 0),
        "antenna_second": draw_antenna_second(jax.random.fold_in(key_list[5], 71), 0),
    }


step_gain = 1.2
penalty_gain = 0.25

def expand_matrix(packed):
    return [[(packed[..., 0, :], packed[..., 1, :]), (packed[..., 2, :], packed[..., 3, :])], [(packed[..., 4, :], packed[..., 5, :]), (packed[..., 6, :], packed[..., 7, :])]]

def pack_matrix(matrix):
    return jnp.stack([matrix[0][0][0], matrix[0][0][1], matrix[0][1][0], matrix[0][1][1], matrix[1][0][0], matrix[1][0][1], matrix[1][1][0], matrix[1][1][1]], axis=-2)

def complex_mul(first_term, second_term):
    return (first_term[0] * second_term[0] - first_term[1] * second_term[1], first_term[0] * second_term[1] + first_term[1] * second_term[0])

def complex_add(first_term, second_term):
    return (first_term[0] + second_term[0], first_term[1] + second_term[1])

def element_of(matrix, i, j, adjoint):
    if adjoint:
        return (matrix[j][i][0], -matrix[j][i][1])
    return matrix[i][j]

def matrix_product(first_factor, second_factor, adjoint_first=False, adjoint_second=False):
    result_rows = []
    for i in range(2):
        row_items = []
        for j in range(2):
            row_items.append(complex_add(complex_mul(element_of(first_factor, i, 0, adjoint_first), element_of(second_factor, 0, j, adjoint_second)), complex_mul(element_of(first_factor, i, 1, adjoint_first), element_of(second_factor, 1, j, adjoint_second))))
        result_rows.append(row_items)
    return result_rows

def fit_basis(band_count):
    positions = (2.0 * jnp.arange(band_count, dtype=jnp.float32) + 1.0) / band_count - 1.0
    columns = []
    for power in range(4):
        vector = positions ** power
        for earlier in columns:
            vector = vector - jnp.sum(earlier * vector) * earlier
        vector = vector / jnp.sqrt(jnp.sum(vector * vector))
        columns.append(vector)
    return jnp.stack(columns, axis=1)

def subband_update(jones_full, coherency_model, visibility_data, antenna_first, antenna_second):
    leading_jones = expand_matrix(jnp.take(jones_full, antenna_first, axis=2))
    trailing_jones = expand_matrix(jnp.take(jones_full, antenna_second, axis=2))
    sky = expand_matrix(coherency_model)
    model = pack_matrix(matrix_product(leading_jones, matrix_product(sky, trailing_jones, adjoint_second=True)))
    residual = visibility_data - lax.optimization_barrier(jnp.sum(model, axis=0))
    resid_parts = expand_matrix(residual[None])
    gradient_leading = pack_matrix(matrix_product(resid_parts, matrix_product(trailing_jones, sky, adjoint_second=True)))
    gradient_trailing = pack_matrix(matrix_product(resid_parts, matrix_product(leading_jones, sky), adjoint_first=True))
    gradient_list = jnp.zeros_like(jones_full).at[:, :, antenna_first].add(gradient_leading).at[:, :, antenna_second].add(gradient_trailing)
    return (gradient_list, residual)

def reference(coherency, observed, jones_deviation, antenna_first, antenna_second):
    highest = lax.Precision.HIGHEST
    baseline_count = coherency.shape[-1]
    station_number = jones_deviation.shape[-1]
    step_size = step_gain * station_number / baseline_count
    penalty = penalty_gain * baseline_count / station_number
    poly_basis = fit_basis(coherency.shape[0])
    identity = jnp.array([1.0, 0.0, 0.0, 0.0, 0.0, 0.0, 1.0, 0.0], dtype=jnp.float32)[:, None]
    jones_current = identity + jones_deviation
    consensus = jones_current
    dual_var = jnp.zeros_like(jones_current)
    residual = None
    for iteration in range(ITERS):
        station_gradients, residual = lax.map(lambda entry_list: subband_update(entry_list[0], entry_list[1], entry_list[2], antenna_first, antenna_second), (jones_current, coherency, observed))
        jones_current = jones_current + step_size * (station_gradients - dual_var - penalty * (jones_current - consensus))
        if iteration + 1 < ITERS:
            target = jones_current + dual_var / penalty
            coefficients = jnp.einsum('fm,fkcs->mkcs', poly_basis, target, precision=highest)
            consensus = jnp.einsum('fm,mkcs->fkcs', poly_basis, coefficients, precision=highest)
            dual_var = dual_var + penalty * (jones_current - consensus)
    return (jones_current, residual)
```

```python
import functools

import jax
import jax.numpy as jnp
import numpy as np
from jax import lax
from jax.experimental import pallas as pl
from jax.experimental.pallas import tpu as pltpu
from jax.sharding import PartitionSpec as P

ITERS = 3
step_gain = 1.2
penalty_gain = 0.25
LANES = 128


def fit_basis(band_count):
    positions = ((2.0 * np.arange(band_count) + 1.0) / band_count - 1.0).astype(np.float32)
    columns = []
    for power in range(4):
        vector = positions**power
        for earlier in columns:
            vector = vector - np.sum(earlier * vector) * earlier
        vector = vector / np.sqrt(np.sum(vector * vector))
        columns.append(vector.astype(np.float32))
    return np.stack(columns, axis=1)


def split(parts):
    return [[(parts[0], parts[1]), (parts[2], parts[3])], [(parts[4], parts[5]), (parts[6], parts[7])]]


def join(matrix):
    return [matrix[i][j][part] for i in range(2) for j in range(2) for part in range(2)]


def element_of(matrix, i, j, adjoint):
    if adjoint:
        return (matrix[j][i][0], -matrix[j][i][1])
    return matrix[i][j]


def product(first, second, adjoint_first=False, adjoint_second=False):
    first, second = split(first), split(second)
    rows = []
    for i in range(2):
        row = []
        for j in range(2):
            a = element_of(first, i, 0, adjoint_first)
            b = element_of(second, 0, j, adjoint_second)
            c = element_of(first, i, 1, adjoint_first)
            d = element_of(second, 1, j, adjoint_second)
            row.append(
                (
                    a[0] * b[0] - a[1] * b[1] + (c[0] * d[0] - c[1] * d[1]),
                    a[0] * b[1] + a[1] * b[0] + (c[0] * d[1] + c[1] * d[0]),
                )
            )
        rows.append(row)
    return join(rows)


def pick(pieces, rows, low, group):
    value = jnp.take_along_axis(pieces[0][rows, :], low, axis=1)
    for j in range(1, 4):
        value = jnp.where(group == j, jnp.take_along_axis(pieces[j][rows, :], low, axis=1), value)
    return value


def iteration_kernel(dirs, core_ref, j0, j1, j2, j3, own_sky, other_sky, seen, place, column, g0, g1, g2, g3, resid, grads, trail, lead):
    core = core_ref[0]
    pieces = (j0, j1, j2, j3)
    half = own_sky.shape[2]
    count = 2 * half
    dir_groups = dirs // 8
    for h in range(count // LANES):
        lanes = slice(h * LANES, (h + 1) * LANES)
        inside = (h * LANES) % half
        first = jnp.broadcast_to(place[0:1, lanes], (8, LANES))
        second = jnp.broadcast_to(place[1:2, lanes], (8, LANES))
        first_low, first_group = first & (LANES - 1), first >> 7
        second_low, second_group = second & (LANES - 1), second >> 7
        total = None
        for g in range(dir_groups):
            rows = [slice(c * dirs + 8 * g, c * dirs + 8 * g + 8) for c in range(8)]
            leading = [pick(pieces, r, first_low, first_group) for r in rows]
            trailing = [pick(pieces, r, second_low, second_group) for r in rows]
            source = own_sky.at[core] if h * LANES < half else other_sky
            sky = [source[r, inside : inside + LANES] for r in rows]
            forward = product(leading, sky)
            model = product(forward, trailing, adjoint_second=True)
            backward = product(trailing, sky, adjoint_second=True)
            for c in range(8):
                lead[rows[c], lanes] = forward[c]
                trail[rows[c], lanes] = backward[c]
            total = model if total is None else [a + b for a, b in zip(total, model)]
        for c in range(8):
            resid[c : c + 1, lanes] = seen[c : c + 1, lanes] - jnp.sum(total[c], axis=0, keepdims=True)
    for h in range(count // LANES):
        lanes = slice(h * LANES, (h + 1) * LANES)
        left = [jnp.broadcast_to(resid[c : c + 1, lanes], (8, LANES)) for c in range(8)]
        for g in range(dir_groups):
            rows = [slice(c * dirs + 8 * g, c * dirs + 8 * g + 8) for c in range(8)]
            up = product(left, [trail[r, lanes] for r in rows])
            down = product(left, [lead[r, lanes] for r in rows], adjoint_first=True)
            for c in range(8):
                grads[rows[c], lanes] = up[c]
                grads[rows[c], count + h * LANES : count + (h + 1) * LANES] = down[c]
    value = grads[...]
    high = value.astype(jnp.bfloat16)
    low = (value - high.astype(jnp.float32)).astype(jnp.bfloat16)
    both = jnp.concatenate([high, low], axis=0)
    where = column[...]
    outs = (g0, g1, g2, g3)
    stations = lax.broadcasted_iota(jnp.int32, (2 * count, 4 * LANES), 1)
    chosen = jnp.where(where == stations, 1.0, 0.0).astype(jnp.bfloat16)
    result = jnp.dot(both, chosen, preferred_element_type=jnp.float32)
    half_rows = value.shape[0]
    result = result[:half_rows] + result[half_rows:]
    for j in range(4):
        outs[j][...] = result[:, j * LANES : (j + 1) * LANES]


def iterate(core, pieces, own_sky, other_sky, seen, place, column):
    rows = pieces[0].shape[0]
    count = place.shape[1]
    dirs = rows // 8
    smem = pl.BlockSpec(memory_space=pltpu.SMEM)
    vmem = pl.BlockSpec(memory_space=pltpu.VMEM)
    piece = jax.ShapeDtypeStruct((rows, LANES), jnp.float32)
    return pl.pallas_call(
        functools.partial(iteration_kernel, dirs),
        out_shape=[piece] * 4 + [jax.ShapeDtypeStruct((8, count), jnp.float32)],
        in_specs=[smem] + [vmem] * 9,
        out_specs=[vmem] * 5,
        scratch_shapes=[
            pltpu.VMEM((rows, 2 * count), jnp.float32),
            pltpu.VMEM((rows, count), jnp.float32),
            pltpu.VMEM((rows, count), jnp.float32),
        ],
        compiler_params=pltpu.CompilerParams(vmem_limit_bytes=32 * 2**20),
        cost_estimate=pl.CostEstimate(flops=4 * 2**27, bytes_accessed=2**21, transcendentals=0),
    )(core, *pieces, own_sky, other_sky, seen, place, column)


def per_device(coherency, observed, jones_deviation, antenna_first, antenna_second):
    base_count = lax.axis_size("base")
    band_count = lax.axis_size("band")
    sub_dev, dirs = coherency.shape[:2]
    base_dev = coherency.shape[-1]
    own_stations = jones_deviation.shape[-1]
    station_number = own_stations * base_count
    baseline_count = base_dev * base_count
    step_size = step_gain * station_number / baseline_count
    penalty = penalty_gain * baseline_count / station_number
    basis = fit_basis(sub_dev * band_count)
    rows = 8 * dirs
    share = rows // 4

    me = lax.axis_index("base")
    core, x, z = me & 1, (me >> 1) & 3, me >> 3
    band = lax.axis_index("band")

    def base_swap(value, mask):
        return lax.ppermute(value, "base", [(i, i ^ mask) for i in range(base_count)])

    def band_swap(value, mask):
        return lax.ppermute(value, "band", [(i, i ^ mask) for i in range(band_count)])

    def along_x(values):
        return [base_swap(values[k - 1], 2 * k) for k in (1, 2, 3)]

    def along_z(values):
        return [base_swap(values[k - 1], 8 * k) for k in (1, 2, 3)]

    def mine_of(value):
        return jnp.where(core == 0, value[0], value[1])

    def theirs_of(value):
        return jnp.where(core == 0, value[1], value[0])

    turned = jones_deviation.transpose(0, 3, 2, 1).reshape(sub_dev, own_stations, rows)
    identity = jnp.repeat(jnp.array([1.0, 0, 0, 0, 0, 0, 1.0, 0], jnp.float32), dirs)
    turned = turned + identity
    mine, theirs = mine_of(turned), base_swap(theirs_of(turned), 1)
    chip = jnp.where(core == 0, jnp.concatenate([mine, theirs]), jnp.concatenate([theirs, mine]))
    planes = [chip] + along_z([chip] * 3)
    ordered = [jnp.where(z & 1 == 0, planes[a], planes[a ^ 1]) for a in range(4)]
    ordered = [jnp.where(z & 2 == 0, ordered[a], ordered[a ^ 2]) for a in range(4)]
    jones = jnp.concatenate(ordered).T

    pairs = jnp.stack([antenna_first, antenna_second])
    pairs = jnp.concatenate([pairs, base_swap(pairs, 1)], axis=1)
    place = ((((pairs >> 5) & 3) ^ x) << 7) | ((pairs >> 7) << 5) | (pairs & 31)
    column = place.reshape(-1, 1)

    sky = coherency.transpose(0, 2, 1, 3).reshape(sub_dev, rows, base_dev)
    other_sky = base_swap(theirs_of(sky), 1)
    seen = jnp.concatenate([mine_of(observed), base_swap(theirs_of(observed), 1)], axis=1)

    share_rows = jnp.arange(rows)[:, None] // share == z
    core_scalar = core.astype(jnp.int32).reshape(1)
    own_basis = lax.dynamic_slice_in_dim(jnp.asarray(basis), 2 * band + core, 1, 0)[0]
    next_basis = lax.dynamic_slice_in_dim(jnp.asarray(basis), 2 * band + 1 - core, 1, 0)[0]
    far_basis = lax.dynamic_slice_in_dim(jnp.asarray(basis), 2 * (band ^ 4) + core, 1, 0)[0]

    def fit(target):
        beside = base_swap(target, 1)
        partial = own_basis[:, None, None] * target + next_basis[:, None, None] * beside
        for mask in (1, 3):
            partial = partial + band_swap(partial, mask)
        sent = band_swap(jnp.sum(far_basis[:, None, None] * partial, axis=0), 4)
        return jnp.sum(own_basis[:, None, None] * partial, axis=0) + sent

    dual = jnp.zeros((share, LANES), jnp.float32)
    correction = None
    residual = None
    for iteration in range(ITERS):
        pieces = [jones] + along_x([jones] * 3)
        *terms, residual = iterate(core_scalar, pieces, sky, other_sky, seen, place, column)
        received = along_x(terms[1:])
        if iteration:
            held = lax.dynamic_slice_in_dim(jones, z * share, share, 0)
            consensus = fit(held + dual / penalty)
            dual = dual + penalty * (held - consensus)
            correction = dual + penalty * (held - consensus)
            spread = jnp.where(share_rows, jnp.concatenate([correction] * 4), 0.0)
            summed = terms[0] - spread + received[0] + received[1] + received[2]
        else:
            summed = terms[0] + received[0] + received[1] + received[2]
        if iteration + 1 < ITERS:
            others = along_z([summed] * 3)
            jones = jones + step_size * (summed + others[0] + others[1] + others[2])
    per_station = 2 * own_stations
    turned_sum = summed.T
    parts = [lax.dynamic_slice_in_dim(turned_sum, (z ^ k) * per_station, per_station, 0) for k in range(4)]
    others = along_z(parts[1:])
    last = lax.dynamic_slice_in_dim(jones.T, z * per_station, per_station, 0)
    last = last + step_size * (parts[0] + others[0] + others[1] + others[2])
    last = last.reshape(2, own_stations, rows)
    kept, given = mine_of(last), base_swap(theirs_of(last), 1)
    both = jnp.where(core == 0, jnp.stack([kept, given]), jnp.stack([given, kept]))
    jones_out = both.reshape(sub_dev, own_stations, 8, dirs).transpose(0, 3, 2, 1)
    here, there = residual[:, :base_dev], base_swap(residual[:, base_dev:], 1)
    residual_out = jnp.where(core == 0, jnp.stack([here, there]), jnp.stack([there, here]))
    return (jones_out, residual_out)


def solution(mesh):
    return jax.shard_map(
        per_device,
        mesh=mesh,
        in_specs=(
            P("band", None, None, "base"),
            P("band", None, "base"),
            P("band", None, None, "base"),
            P("base"),
            P("base"),
        ),
        out_specs=(P("band", None, None, "base"), P("band", None, "base")),
        check_vma=False,
    )
```

```python
import functools

import jax
import jax.numpy as jnp
import numpy as np
from jax import lax
from jax.experimental import pallas as pl
from jax.experimental.pallas import tpu as pltpu
from jax.sharding import PartitionSpec as P

ITERS = 3
step_gain = 1.2
penalty_gain = 0.25
LANES = 128


def fit_basis(band_count):
    positions = ((2.0 * np.arange(band_count) + 1.0) / band_count - 1.0).astype(np.float32)
    columns = []
    for power in range(4):
        vector = positions**power
        for earlier in columns:
            vector = vector - np.sum(earlier * vector) * earlier
        vector = vector / np.sqrt(np.sum(vector * vector))
        columns.append(vector.astype(np.float32))
    return np.stack(columns, axis=1)


def fit_table(basis, sub_dev, band_count):
    project = basis @ basis.T
    table = np.zeros((sub_dev * band_count, 16), np.float32)
    for band in range(band_count):
        for core in range(sub_dev):
            for to in range(4):
                target = 2 * (band ^ to) + core
                sources = [2 * band + core, 2 * (band ^ 4) + core, 2 * band + (core ^ 1), 2 * (band ^ 4) + (core ^ 1)]
                table[2 * band + core, to::4] = project[target, sources]
    return table


def split(parts):
    return [[(parts[0], parts[1]), (parts[2], parts[3])], [(parts[4], parts[5]), (parts[6], parts[7])]]


def join(matrix):
    return [matrix[i][j][part] for i in range(2) for j in range(2) for part in range(2)]


def element_of(matrix, i, j, adjoint):
    if adjoint:
        return (matrix[j][i][0], -matrix[j][i][1])
    return matrix[i][j]


def product(first, second, adjoint_first=False, adjoint_second=False):
    first, second = split(first), split(second)
    rows = []
    for i in range(2):
        row = []
        for j in range(2):
            a = element_of(first, i, 0, adjoint_first)
            b = element_of(second, 0, j, adjoint_second)
            c = element_of(first, i, 1, adjoint_first)
            d = element_of(second, 1, j, adjoint_second)
            row.append(
                (
                    a[0] * b[0] - a[1] * b[1] + (c[0] * d[0] - c[1] * d[1]),
                    a[0] * b[1] + a[1] * b[0] + (c[0] * d[1] + c[1] * d[0]),
                )
            )
        rows.append(row)
    return join(rows)


def pick(pieces, rows, low, group):
    value = jnp.take_along_axis(pieces[0][rows, :], low, axis=1)
    for j in range(1, 4):
        value = jnp.where(group == j, jnp.take_along_axis(pieces[j][rows, :], low, axis=1), value)
    return value


def iteration_kernel(dirs, core_ref, j0, j1, j2, j3, own_sky, other_sky, seen, place, column, g0, g1, g2, g3, resid, grads, trail, lead):
    core = core_ref[0]
    pieces = (j0, j1, j2, j3)
    half = own_sky.shape[2]
    count = 2 * half
    dir_groups = dirs // 8
    for h in range(count // LANES):
        lanes = slice(h * LANES, (h + 1) * LANES)
        inside = (h * LANES) % half
        first = jnp.broadcast_to(place[0:1, lanes], (8, LANES))
        second = jnp.broadcast_to(place[1:2, lanes], (8, LANES))
        first_low, first_group = first & (LANES - 1), first >> 7
        second_low, second_group = second & (LANES - 1), second >> 7
        total = None
        for g in range(dir_groups):
            rows = [slice(c * dirs + 8 * g, c * dirs + 8 * g + 8) for c in range(8)]
            leading = [pick(pieces, r, first_low, first_group) for r in rows]
            trailing = [pick(pieces, r, second_low, second_group) for r in rows]
            source = own_sky.at[core] if h * LANES < half else other_sky
            sky = [source[r, inside : inside + LANES] for r in rows]
            forward = product(leading, sky)
            model = product(forward, trailing, adjoint_second=True)
            backward = product(trailing, sky, adjoint_second=True)
            for c in range(8):
                lead[rows[c], lanes] = forward[c]
                trail[rows[c], lanes] = backward[c]
            total = model if total is None else [a + b for a, b in zip(total, model)]
        for c in range(8):
            resid[c : c + 1, lanes] = seen[c : c + 1, lanes] - jnp.sum(total[c], axis=0, keepdims=True)
    for h in range(count // LANES):
        lanes = slice(h * LANES, (h + 1) * LANES)
        left = [jnp.broadcast_to(resid[c : c + 1, lanes], (8, LANES)) for c in range(8)]
        for g in range(dir_groups):
            rows = [slice(c * dirs + 8 * g, c * dirs + 8 * g + 8) for c in range(8)]
            up = product(left, [trail[r, lanes] for r in rows])
            down = product(left, [lead[r, lanes] for r in rows], adjoint_first=True)
            for c in range(8):
                grads[rows[c], lanes] = up[c]
                grads[rows[c], count + h * LANES : count + (h + 1) * LANES] = down[c]
    value = grads[...]
    high = value.astype(jnp.bfloat16)
    low = (value - high.astype(jnp.float32)).astype(jnp.bfloat16)
    both = jnp.concatenate([high, low], axis=0)
    where = column[...]
    outs = (g0, g1, g2, g3)
    stations = lax.broadcasted_iota(jnp.int32, (2 * count, 4 * LANES), 1)
    chosen = jnp.where(where == stations, 1.0, 0.0).astype(jnp.bfloat16)
    result = jnp.dot(both, chosen, preferred_element_type=jnp.float32)
    half_rows = value.shape[0]
    result = result[:half_rows] + result[half_rows:]
    for j in range(4):
        outs[j][...] = result[:, j * LANES : (j + 1) * LANES]


def iterate(core, pieces, own_sky, other_sky, seen, place, column):
    rows = pieces[0].shape[0]
    count = place.shape[1]
    dirs = rows // 8
    smem = pl.BlockSpec(memory_space=pltpu.SMEM)
    vmem = pl.BlockSpec(memory_space=pltpu.VMEM)
    piece = jax.ShapeDtypeStruct((rows, LANES), jnp.float32)
    return pl.pallas_call(
        functools.partial(iteration_kernel, dirs),
        out_shape=[piece] * 4 + [jax.ShapeDtypeStruct((8, count), jnp.float32)],
        in_specs=[smem] + [vmem] * 9,
        out_specs=[vmem] * 5,
        scratch_shapes=[
            pltpu.VMEM((rows, 2 * count), jnp.float32),
            pltpu.VMEM((rows, count), jnp.float32),
            pltpu.VMEM((rows, count), jnp.float32),
        ],
        compiler_params=pltpu.CompilerParams(vmem_limit_bytes=32 * 2**20),
        cost_estimate=pl.CostEstimate(flops=4 * 2**27, bytes_accessed=2**21, transcendentals=0),
    )(core, *pieces, own_sky, other_sky, seen, place, column)


def per_device(coherency, observed, jones_deviation, antenna_first, antenna_second):
    base_count = lax.axis_size("base")
    band_count = lax.axis_size("band")
    sub_dev, dirs = coherency.shape[:2]
    base_dev = coherency.shape[-1]
    own_stations = jones_deviation.shape[-1]
    station_number = own_stations * base_count
    baseline_count = base_dev * base_count
    step_size = step_gain * station_number / baseline_count
    penalty = penalty_gain * baseline_count / station_number
    basis = fit_basis(sub_dev * band_count)
    rows = 8 * dirs

    me = lax.axis_index("base")
    core, x, z = me & 1, (me >> 1) & 3, me >> 3
    band = lax.axis_index("band")

    def base_swap(value, mask):
        return lax.ppermute(value, "base", [(i, i ^ mask) for i in range(base_count)])

    def band_swap(value, mask):
        return lax.ppermute(value, "band", [(i, i ^ mask) for i in range(band_count)])

    def along_x(values):
        return [base_swap(values[k - 1], 2 * k) for k in (1, 2, 3)]

    def along_z(values):
        return [base_swap(values[k - 1], 8 * k) for k in (1, 2, 3)]

    def mine_of(value):
        return jnp.where(core == 0, value[0], value[1])

    def theirs_of(value):
        return jnp.where(core == 0, value[1], value[0])

    plane_groups = [[8 * a + 2 * b + c for a in range(4) for b in range(4)] for c in range(2)]

    def exchange(value):
        return lax.all_to_all(value, "base", 0, 0, axis_index_groups=plane_groups, tiled=True)

    def reorder(quarters):
        quarters = [jnp.where(x & 1 == 0, quarters[a], quarters[a ^ 1]) for a in range(4)]
        return [jnp.where(x & 2 == 0, quarters[a], quarters[a ^ 2]) for a in range(4)]

    turned = jones_deviation.transpose(0, 3, 2, 1).reshape(sub_dev, own_stations, rows)
    mine, theirs = mine_of(turned), base_swap(theirs_of(turned), 1)
    chip = jnp.where(core == 0, jnp.concatenate([mine, theirs]), jnp.concatenate([theirs, mine]))
    gathered = exchange(jnp.broadcast_to(chip, (16, *chip.shape)).reshape(-1, rows)).reshape(4, 4, 2 * own_stations, rows)
    component = jnp.arange(rows)[:, None] // dirs
    identity = jnp.where((component == 0) | (component == 6), 1.0, 0.0).astype(jnp.float32)
    pieces = [q.reshape(LANES, rows).T + identity for q in reorder([gathered[:, a] for a in range(4)])]
    jones = pieces[0]

    pairs = jnp.stack([antenna_first, antenna_second])
    pairs = jnp.concatenate([pairs, base_swap(pairs, 1)], axis=1)
    place = ((((pairs >> 5) & 3) ^ x) << 7) | ((pairs >> 7) << 5) | (pairs & 31)
    column = place.reshape(-1, 1)

    sky = coherency.transpose(0, 2, 1, 3).reshape(sub_dev, rows, base_dev)
    other_sky = base_swap(theirs_of(sky), 1)
    seen = jnp.concatenate([mine_of(observed), base_swap(theirs_of(observed), 1)], axis=1)

    core_scalar = core.astype(jnp.int32).reshape(1)
    table = fit_table(basis, sub_dev, band_count)
    weights = lax.dynamic_slice_in_dim(jnp.asarray(table), 2 * band + core, 1, 0)[0].reshape(4, 4)
    both_axes = ("base", "band")

    across_z = [
        (i * band_count + j, (i ^ 24) * band_count + (j ^ 4)) for i in range(base_count) for j in range(band_count)
    ]

    def after(value, *others):
        return lax.optimization_barrier((value, *others))[0]

    jones, weights = lax.optimization_barrier((jones, tuple(weights[k] for k in range(4))))
    dual = jnp.zeros((rows, LANES), jnp.float32)
    residual = None
    for iteration in range(ITERS):
        if iteration:
            pieces = [jones] + along_x([jones] * 3)
            target = jones + dual / penalty
            pair = jnp.stack([target, lax.ppermute(target, both_axes, across_z)])
            pair = after(pair, *pieces[1:]) if True else pair
            four = [*pair, *base_swap(pair, 1)]
            meant = sum(weights[k][:, None, None] * four[k] for k in range(4))
        *terms, residual = iterate(core_scalar, pieces, sky, other_sky, seen, place, column)
        last_one = iteration + 1 == ITERS
        received = None if last_one else along_x(terms[1:])
        if iteration:
            sent = meant[1:3]
            if 1 == 1:
                sent = after(sent, terms[0])
            elif 1 == 2 and not last_one:
                sent = after(sent, *received)
            came = band_swap(sent, 1)
            further = meant[3] + came[1]
            if 0 == 1 and not last_one:
                further = after(further, *received)
            consensus = meant[0] + came[0] + band_swap(further, 3)
            dual = dual + penalty * (jones - consensus)
            jones_next = jones - step_size * (dual + penalty * (jones - consensus))
        else:
            jones_next = jones
        if not last_one:
            summed = terms[0] + received[0] + received[1] + received[2]
            others = along_z([summed] * 3)
            jones = jones_next + step_size * (summed + others[0] + others[1] + others[2])
    per_station = 2 * own_stations
    leaving = jnp.stack([q.T.reshape(4, per_station, rows) for q in reorder(terms)], axis=1)
    came = exchange(leaving.reshape(16 * per_station, rows)).reshape(16, per_station, rows)
    last = lax.dynamic_slice_in_dim(jones_next.T, z * per_station, per_station, 0)
    last = last + step_size * jnp.sum(came, axis=0)
    last = last.reshape(2, own_stations, rows)
    kept, given = mine_of(last), base_swap(theirs_of(last), 1)
    both = jnp.where(core == 0, jnp.stack([kept, given]), jnp.stack([given, kept]))
    jones_out = both.reshape(sub_dev, own_stations, 8, dirs).transpose(0, 3, 2, 1)
    here, there = residual[:, :base_dev], base_swap(residual[:, base_dev:], 1)
    residual_out = jnp.where(core == 0, jnp.stack([here, there]), jnp.stack([there, here]))
    return (jones_out, residual_out)


def solution(mesh):
    return jax.shard_map(
        per_device,
        mesh=mesh,
        in_specs=(
            P("band", None, None, "base"),
            P("band", None, "base"),
            P("band", None, None, "base"),
            P("base"),
            P("base"),
        ),
        out_specs=(P("band", None, None, "base"), P("band", None, "base")),
        check_vma=False,
    )
```

```python
import functools

import jax
import jax.numpy as jnp
import numpy as np
from jax import lax
from jax.experimental import pallas as pl
from jax.experimental.pallas import tpu as pltpu
from jax.sharding import PartitionSpec as P

ITERS = 3
step_gain = 1.2
penalty_gain = 0.25
LANES = 128


def fit_basis(band_count):
    positions = ((2.0 * np.arange(band_count) + 1.0) / band_count - 1.0).astype(np.float32)
    columns = []
    for power in range(4):
        vector = positions**power
        for earlier in columns:
            vector = vector - np.sum(earlier * vector) * earlier
        vector = vector / np.sqrt(np.sum(vector * vector))
        columns.append(vector.astype(np.float32))
    return np.stack(columns, axis=1)


def fit_table(basis, sub_dev, band_count):
    project = basis @ basis.T
    table = np.zeros((sub_dev * band_count, 16), np.float32)
    for band in range(band_count):
        for core in range(sub_dev):
            for to in range(4):
                target = 2 * (band ^ to) + core
                sources = [2 * band + core, 2 * (band ^ 4) + core, 2 * band + (core ^ 1), 2 * (band ^ 4) + (core ^ 1)]
                table[2 * band + core, to::4] = project[target, sources]
    return table


def split(parts):
    return [[(parts[0], parts[1]), (parts[2], parts[3])], [(parts[4], parts[5]), (parts[6], parts[7])]]


def join(matrix):
    return [matrix[i][j][part] for i in range(2) for j in range(2) for part in range(2)]


def element_of(matrix, i, j, adjoint):
    if adjoint:
        return (matrix[j][i][0], -matrix[j][i][1])
    return matrix[i][j]


def product(first, second, adjoint_first=False, adjoint_second=False):
    first, second = split(first), split(second)
    rows = []
    for i in range(2):
        row = []
        for j in range(2):
            a = element_of(first, i, 0, adjoint_first)
            b = element_of(second, 0, j, adjoint_second)
            c = element_of(first, i, 1, adjoint_first)
            d = element_of(second, 1, j, adjoint_second)
            row.append(
                (
                    a[0] * b[0] - a[1] * b[1] + (c[0] * d[0] - c[1] * d[1]),
                    a[0] * b[1] + a[1] * b[0] + (c[0] * d[1] + c[1] * d[0]),
                )
            )
        rows.append(row)
    return join(rows)


def pick(pieces, rows, low, group):
    value = jnp.take_along_axis(pieces[0][rows, :], low, axis=1)
    for j in range(1, 4):
        value = jnp.where(group == j, jnp.take_along_axis(pieces[j][rows, :], low, axis=1), value)
    return value


def iteration_kernel(dirs, core_ref, j0, j1, j2, j3, own_sky, other_sky, seen, place, column, g0, g1, g2, g3, resid, grads, trail, lead):
    core = core_ref[0]
    pieces = (j0, j1, j2, j3)
    half = own_sky.shape[2]
    count = 2 * half
    dir_groups = dirs // 8
    for h in range(count // LANES):
        lanes = slice(h * LANES, (h + 1) * LANES)
        inside = (h * LANES) % half
        first = jnp.broadcast_to(place[0:1, lanes], (8, LANES))
        second = jnp.broadcast_to(place[1:2, lanes], (8, LANES))
        first_low, first_group = first & (LANES - 1), first >> 7
        second_low, second_group = second & (LANES - 1), second >> 7
        total = None
        for g in range(dir_groups):
            rows = [slice(c * dirs + 8 * g, c * dirs + 8 * g + 8) for c in range(8)]
            leading = [pick(pieces, r, first_low, first_group) for r in rows]
            trailing = [pick(pieces, r, second_low, second_group) for r in rows]
            source = own_sky.at[core] if h * LANES < half else other_sky
            sky = [source[r, inside : inside + LANES] for r in rows]
            forward = product(leading, sky)
            model = product(forward, trailing, adjoint_second=True)
            backward = product(trailing, sky, adjoint_second=True)
            for c in range(8):
                lead[rows[c], lanes] = forward[c]
                trail[rows[c], lanes] = backward[c]
            total = model if total is None else [a + b for a, b in zip(total, model)]
        for c in range(8):
            resid[c : c + 1, lanes] = seen[c : c + 1, lanes] - jnp.sum(total[c], axis=0, keepdims=True)
    for h in range(count // LANES):
        lanes = slice(h * LANES, (h + 1) * LANES)
        left = [jnp.broadcast_to(resid[c : c + 1, lanes], (8, LANES)) for c in range(8)]
        for g in range(dir_groups):
            rows = [slice(c * dirs + 8 * g, c * dirs + 8 * g + 8) for c in range(8)]
            up = product(left, [trail[r, lanes] for r in rows])
            down = product(left, [lead[r, lanes] for r in rows], adjoint_first=True)
            for c in range(8):
                grads[rows[c], lanes] = up[c]
                grads[rows[c], count + h * LANES : count + (h + 1) * LANES] = down[c]
    value = grads[...]
    high = value.astype(jnp.bfloat16)
    low = (value - high.astype(jnp.float32)).astype(jnp.bfloat16)
    both = jnp.concatenate([high, low], axis=0)
    where = column[...]
    outs = (g0, g1, g2, g3)
    stations = lax.broadcasted_iota(jnp.int32, (2 * count, 4 * LANES), 1)
    chosen = jnp.where(where == stations, 1.0, 0.0).astype(jnp.bfloat16)
    result = jnp.dot(both, chosen, preferred_element_type=jnp.float32)
    half_rows = value.shape[0]
    result = result[:half_rows] + result[half_rows:]
    for j in range(4):
        outs[j][...] = result[:, j * LANES : (j + 1) * LANES]


def iterate(core, pieces, own_sky, other_sky, seen, place, column):
    rows = pieces[0].shape[0]
    count = place.shape[1]
    dirs = rows // 8
    smem = pl.BlockSpec(memory_space=pltpu.SMEM)
    vmem = pl.BlockSpec(memory_space=pltpu.VMEM)
    piece = jax.ShapeDtypeStruct((rows, LANES), jnp.float32)
    return pl.pallas_call(
        functools.partial(iteration_kernel, dirs),
        out_shape=[piece] * 4 + [jax.ShapeDtypeStruct((8, count), jnp.float32)],
        in_specs=[smem] + [vmem] * 9,
        out_specs=[vmem] * 5,
        scratch_shapes=[
            pltpu.VMEM((rows, 2 * count), jnp.float32),
            pltpu.VMEM((rows, count), jnp.float32),
            pltpu.VMEM((rows, count), jnp.float32),
        ],
        compiler_params=pltpu.CompilerParams(vmem_limit_bytes=32 * 2**20),
        cost_estimate=pl.CostEstimate(flops=4 * 2**27, bytes_accessed=2**21, transcendentals=0),
    )(core, *pieces, own_sky, other_sky, seen, place, column)


def per_device(coherency, observed, jones_deviation, antenna_first, antenna_second):
    base_count = lax.axis_size("base")
    band_count = lax.axis_size("band")
    sub_dev, dirs = coherency.shape[:2]
    base_dev = coherency.shape[-1]
    own_stations = jones_deviation.shape[-1]
    station_number = own_stations * base_count
    baseline_count = base_dev * base_count
    step_size = step_gain * station_number / baseline_count
    penalty = penalty_gain * baseline_count / station_number
    basis = fit_basis(sub_dev * band_count)
    rows = 8 * dirs

    me = lax.axis_index("base")
    core, x, z = me & 1, (me >> 1) & 3, me >> 3
    band = lax.axis_index("band")

    def base_swap(value, mask):
        return lax.ppermute(value, "base", [(i, i ^ mask) for i in range(base_count)])

    def band_swap(value, mask):
        return lax.ppermute(value, "band", [(i, i ^ mask) for i in range(band_count)])

    def along_x(values):
        return [base_swap(values[k - 1], 2 * k) for k in (1, 2, 3)]

    def along_z(values):
        return [base_swap(values[k - 1], 8 * k) for k in (1, 2, 3)]

    def mine_of(value):
        return jnp.where(core == 0, value[0], value[1])

    def theirs_of(value):
        return jnp.where(core == 0, value[1], value[0])

    plane_groups = [[8 * a + 2 * b + c for a in range(4) for b in range(4)] for c in range(2)]

    def exchange(value):
        return lax.all_to_all(value, "base", 0, 0, axis_index_groups=plane_groups, tiled=True)

    def reorder(quarters):
        quarters = [jnp.where(x & 1 == 0, quarters[a], quarters[a ^ 1]) for a in range(4)]
        return [jnp.where(x & 2 == 0, quarters[a], quarters[a ^ 2]) for a in range(4)]

    turned = jones_deviation.transpose(0, 3, 2, 1).reshape(sub_dev, own_stations, rows)
    mine, theirs = mine_of(turned), base_swap(theirs_of(turned), 1)
    chip = jnp.where(core == 0, jnp.concatenate([mine, theirs]), jnp.concatenate([theirs, mine]))
    gathered = exchange(jnp.broadcast_to(chip, (16, *chip.shape)).reshape(-1, rows)).reshape(4, 4, 2 * own_stations, rows)
    component = jnp.arange(rows)[:, None] // dirs
    identity = jnp.where((component == 0) | (component == 6), 1.0, 0.0).astype(jnp.float32)
    pieces = [q.reshape(LANES, rows).T + identity for q in reorder([gathered[:, a] for a in range(4)])]
    jones = pieces[0]

    antenna_first, antenna_second, coherency, observed = lax.optimization_barrier(
        (antenna_first, antenna_second, coherency, observed, theirs)
    )[:4]
    pairs = jnp.stack([antenna_first, antenna_second])
    pairs = jnp.concatenate([pairs, base_swap(pairs, 1)], axis=1)
    place = ((((pairs >> 5) & 3) ^ x) << 7) | ((pairs >> 7) << 5) | (pairs & 31)
    column = place.reshape(-1, 1)

    sky = coherency.transpose(0, 2, 1, 3).reshape(sub_dev, rows, base_dev)
    other_sky = base_swap(theirs_of(sky), 1)
    seen = jnp.concatenate([mine_of(observed), base_swap(theirs_of(observed), 1)], axis=1)

    core_scalar = core.astype(jnp.int32).reshape(1)
    table = fit_table(basis, sub_dev, band_count)
    weights = lax.dynamic_slice_in_dim(jnp.asarray(table), 2 * band + core, 1, 0)[0].reshape(4, 4)
    both_axes = ("base", "band")

    across_z = [
        (i * band_count + j, (i ^ 24) * band_count + (j ^ 4)) for i in range(base_count) for j in range(band_count)
    ]

    def after(value, *others):
        return lax.optimization_barrier((value, *others))[0]

    jones, weights = lax.optimization_barrier((jones, tuple(weights[k] for k in range(4))))
    dual = jnp.zeros((rows, LANES), jnp.float32)
    residual = None
    for iteration in range(ITERS):
        if iteration:
            pieces = [jones] + along_x([jones] * 3)
            target = jones + dual / penalty
            pair = jnp.stack([target, lax.ppermute(target, both_axes, across_z)])
            pair = after(pair, *pieces[1:])
            four = [*pair, *base_swap(pair, 1)]
            meant = sum(weights[k][:, None, None] * four[k] for k in range(4))
        *terms, residual = iterate(core_scalar, pieces, sky, other_sky, seen, place, column)
        last_one = iteration + 1 == ITERS
        if last_one:
            terms, meant = lax.optimization_barrier((terms, meant))
        received = along_x(terms[1:])
        if iteration:
            came = band_swap(after(meant[1:3], terms[0]), 1)
            further = meant[3] + came[1]
            consensus = meant[0] + came[0] + band_swap(further, 3)
            dual = dual + penalty * (jones - consensus)
            jones_next = jones - step_size * (dual + penalty * (jones - consensus))
        else:
            jones_next = jones
        summed = terms[0] + received[0] + received[1] + received[2]
        if not last_one:
            others = along_z([summed] * 3)
            jones = jones_next + step_size * (summed + others[0] + others[1] + others[2])
    per_station = 2 * own_stations
    here, there = residual[:, :base_dev], base_swap(residual[:, base_dev:], 1)
    residual_out = jnp.where(core == 0, jnp.stack([here, there]), jnp.stack([there, here]))
    turned_sum = summed.T
    parts = [lax.dynamic_slice_in_dim(turned_sum, (z ^ k) * per_station, per_station, 0) for k in range(4)]
    others = along_z(parts[1:])
    residual_out, others = lax.optimization_barrier((residual_out, others))
    last = lax.dynamic_slice_in_dim(jones_next.T, z * per_station, per_station, 0)
    last = last + step_size * (parts[0] + others[0] + others[1] + others[2])
    last = last.reshape(2, own_stations, rows)
    kept, given = mine_of(last), base_swap(theirs_of(last), 1)
    both = jnp.where(core == 0, jnp.stack([kept, given]), jnp.stack([given, kept]))
    jones_out = both.reshape(sub_dev, own_stations, 8, dirs).transpose(0, 3, 2, 1)
    return (jones_out, residual_out)


def solution(mesh):
    return jax.shard_map(
        per_device,
        mesh=mesh,
        in_specs=(
            P("band", None, None, "base"),
            P("band", None, "base"),
            P("band", None, None, "base"),
            P("base"),
            P("base"),
        ),
        out_specs=(P("band", None, None, "base"), P("band", None, "base")),
        check_vma=False,
    )
```

```python
import functools

import jax
import jax.numpy as jnp
import numpy as np
from jax import lax
from jax.experimental import pallas as pl
from jax.experimental.pallas import tpu as pltpu
from jax.sharding import PartitionSpec as P

ITERS = 3
step_gain = 1.2
penalty_gain = 0.25
LANES = 128


def fit_basis(band_count):
    positions = ((2.0 * np.arange(band_count) + 1.0) / band_count - 1.0).astype(np.float32)
    columns = []
    for power in range(4):
        vector = positions**power
        for earlier in columns:
            vector = vector - np.sum(earlier * vector) * earlier
        vector = vector / np.sqrt(np.sum(vector * vector))
        columns.append(vector.astype(np.float32))
    return np.stack(columns, axis=1)


def fit_table(basis, sub_dev, band_count):
    project = basis @ basis.T
    table = np.zeros((sub_dev * band_count, 16), np.float32)
    for band in range(band_count):
        for core in range(sub_dev):
            for to in range(4):
                target = 2 * (band ^ to) + core
                sources = [2 * band + core, 2 * (band ^ 4) + core, 2 * band + (core ^ 1), 2 * (band ^ 4) + (core ^ 1)]
                table[2 * band + core, to::4] = project[target, sources]
    return table


def split(parts):
    return [[(parts[0], parts[1]), (parts[2], parts[3])], [(parts[4], parts[5]), (parts[6], parts[7])]]


def join(matrix):
    return [matrix[i][j][part] for i in range(2) for j in range(2) for part in range(2)]


def element_of(matrix, i, j, adjoint):
    if adjoint:
        return (matrix[j][i][0], -matrix[j][i][1])
    return matrix[i][j]


def product(first, second, adjoint_first=False, adjoint_second=False):
    first, second = split(first), split(second)
    rows = []
    for i in range(2):
        row = []
        for j in range(2):
            a = element_of(first, i, 0, adjoint_first)
            b = element_of(second, 0, j, adjoint_second)
            c = element_of(first, i, 1, adjoint_first)
            d = element_of(second, 1, j, adjoint_second)
            row.append(
                (
                    a[0] * b[0] - a[1] * b[1] + (c[0] * d[0] - c[1] * d[1]),
                    a[0] * b[1] + a[1] * b[0] + (c[0] * d[1] + c[1] * d[0]),
                )
            )
        rows.append(row)
    return join(rows)


def pick(pieces, rows, low, group):
    value = jnp.take_along_axis(pieces[0][rows, :], low, axis=1)
    for j in range(1, 4):
        value = jnp.where(group == j, jnp.take_along_axis(pieces[j][rows, :], low, axis=1), value)
    return value


def iteration_kernel(dirs, core_ref, j0, j1, j2, j3, own_sky, other_sky, seen, place, column, g0, g1, g2, g3, resid, grads, trail, lead):
    core = core_ref[0]
    pieces = (j0, j1, j2, j3)
    half = own_sky.shape[2]
    count = 2 * half
    dir_groups = dirs // 8
    for h in range(count // LANES):
        lanes = slice(h * LANES, (h + 1) * LANES)
        inside = (h * LANES) % half
        first = jnp.broadcast_to(place[0:1, lanes], (8, LANES))
        second = jnp.broadcast_to(place[1:2, lanes], (8, LANES))
        first_low, first_group = first & (LANES - 1), first >> 7
        second_low, second_group = second & (LANES - 1), second >> 7
        total = None
        for g in range(dir_groups):
            rows = [slice(c * dirs + 8 * g, c * dirs + 8 * g + 8) for c in range(8)]
            leading = [pick(pieces, r, first_low, first_group) for r in rows]
            trailing = [pick(pieces, r, second_low, second_group) for r in rows]
            source = own_sky.at[core] if h * LANES < half else other_sky
            sky = [source[r, inside : inside + LANES] for r in rows]
            forward = product(leading, sky)
            model = product(forward, trailing, adjoint_second=True)
            backward = product(trailing, sky, adjoint_second=True)
            for c in range(8):
                lead[rows[c], lanes] = forward[c]
                trail[rows[c], lanes] = backward[c]
            total = model if total is None else [a + b for a, b in zip(total, model)]
        for c in range(8):
            resid[c : c + 1, lanes] = seen[c : c + 1, lanes] - jnp.sum(total[c], axis=0, keepdims=True)
    for h in range(count // LANES):
        lanes = slice(h * LANES, (h + 1) * LANES)
        left = [jnp.broadcast_to(resid[c : c + 1, lanes], (8, LANES)) for c in range(8)]
        for g in range(dir_groups):
            rows = [slice(c * dirs + 8 * g, c * dirs + 8 * g + 8) for c in range(8)]
            up = product(left, [trail[r, lanes] for r in rows])
            down = product(left, [lead[r, lanes] for r in rows], adjoint_first=True)
            for c in range(8):
                grads[rows[c], lanes] = up[c]
                grads[rows[c], count + h * LANES : count + (h + 1) * LANES] = down[c]
    value = grads[...]
    high = value.astype(jnp.bfloat16)
    low = (value - high.astype(jnp.float32)).astype(jnp.bfloat16)
    both = jnp.concatenate([high, low], axis=0)
    where = column[...]
    outs = (g0, g1, g2, g3)
    stations = lax.broadcasted_iota(jnp.int32, (2 * count, 4 * LANES), 1)
    chosen = jnp.where(where == stations, 1.0, 0.0).astype(jnp.bfloat16)
    result = jnp.dot(both, chosen, preferred_element_type=jnp.float32)
    half_rows = value.shape[0]
    result = result[:half_rows] + result[half_rows:]
    for j in range(4):
        outs[j][...] = result[:, j * LANES : (j + 1) * LANES]


def iterate(core, pieces, own_sky, other_sky, seen, place, column):
    rows = pieces[0].shape[0]
    count = place.shape[1]
    dirs = rows // 8
    smem = pl.BlockSpec(memory_space=pltpu.SMEM)
    vmem = pl.BlockSpec(memory_space=pltpu.VMEM)
    piece = jax.ShapeDtypeStruct((rows, LANES), jnp.float32)
    return pl.pallas_call(
        functools.partial(iteration_kernel, dirs),
        out_shape=[piece] * 4 + [jax.ShapeDtypeStruct((8, count), jnp.float32)],
        in_specs=[smem] + [vmem] * 9,
        out_specs=[vmem] * 5,
        scratch_shapes=[
            pltpu.VMEM((rows, 2 * count), jnp.float32),
            pltpu.VMEM((rows, count), jnp.float32),
            pltpu.VMEM((rows, count), jnp.float32),
        ],
        compiler_params=pltpu.CompilerParams(vmem_limit_bytes=32 * 2**20),
        cost_estimate=pl.CostEstimate(flops=4 * 2**27, bytes_accessed=2**21, transcendentals=0),
    )(core, *pieces, own_sky, other_sky, seen, place, column)


def per_device(coherency, observed, jones_deviation, antenna_first, antenna_second):
    base_count = lax.axis_size("base")
    band_count = lax.axis_size("band")
    sub_dev, dirs = coherency.shape[:2]
    base_dev = coherency.shape[-1]
    own_stations = jones_deviation.shape[-1]
    station_number = own_stations * base_count
    baseline_count = base_dev * base_count
    step_size = step_gain * station_number / baseline_count
    penalty = penalty_gain * baseline_count / station_number
    basis = fit_basis(sub_dev * band_count)
    rows = 8 * dirs

    me = lax.axis_index("base")
    core, x, z = me & 1, (me >> 1) & 3, me >> 3
    band = lax.axis_index("band")

    def base_swap(value, mask):
        return lax.ppermute(value, "base", [(i, i ^ mask) for i in range(base_count)])

    def band_swap(value, mask):
        return lax.ppermute(value, "band", [(i, i ^ mask) for i in range(band_count)])

    def along_x(values):
        return [base_swap(values[k - 1], 2 * k) for k in (1, 2, 3)]

    def along_z(values):
        return [base_swap(values[k - 1], 8 * k) for k in (1, 2, 3)]

    def mine_of(value):
        return jnp.where(core == 0, value[0], value[1])

    def theirs_of(value):
        return jnp.where(core == 0, value[1], value[0])

    plane_groups = [[8 * a + 2 * b + c for a in range(4) for b in range(4)] for c in range(2)]

    def exchange(value):
        return lax.all_to_all(value, "base", 0, 0, axis_index_groups=plane_groups, tiled=True)

    def reorder(quarters):
        quarters = [jnp.where(x & 1 == 0, quarters[a], quarters[a ^ 1]) for a in range(4)]
        return [jnp.where(x & 2 == 0, quarters[a], quarters[a ^ 2]) for a in range(4)]

    turned = jones_deviation.transpose(0, 3, 2, 1).reshape(sub_dev, own_stations, rows)
    mine, theirs = mine_of(turned), base_swap(theirs_of(turned), 1)
    chip = jnp.where(core == 0, jnp.concatenate([mine, theirs]), jnp.concatenate([theirs, mine]))
    gathered = exchange(jnp.broadcast_to(chip, (16, *chip.shape)).reshape(-1, rows)).reshape(4, 4, 2 * own_stations, rows)
    component = jnp.arange(rows)[:, None] // dirs
    identity = jnp.where((component == 0) | (component == 6), 1.0, 0.0).astype(jnp.float32)
    pieces = [q.reshape(LANES, rows).T + identity for q in reorder([gathered[:, a] for a in range(4)])]
    jones = pieces[0]

    antenna_first, antenna_second, coherency, observed = lax.optimization_barrier(
        (antenna_first, antenna_second, coherency, observed, theirs)
    )[:4]
    pairs = jnp.stack([antenna_first, antenna_second])
    pairs = jnp.concatenate([pairs, base_swap(pairs, 1)], axis=1)
    place = ((((pairs >> 5) & 3) ^ x) << 7) | ((pairs >> 7) << 5) | (pairs & 31)
    column = place.reshape(-1, 1)

    sky = coherency.transpose(0, 2, 1, 3).reshape(sub_dev, rows, base_dev)
    other_sky = base_swap(theirs_of(sky), 1)
    seen = jnp.concatenate([mine_of(observed), base_swap(theirs_of(observed), 1)], axis=1)

    core_scalar = core.astype(jnp.int32).reshape(1)
    table = fit_table(basis, sub_dev, band_count)
    weights = lax.dynamic_slice_in_dim(jnp.asarray(table), 2 * band + core, 1, 0)[0].reshape(4, 4)
    both_axes = ("base", "band")

    across_z = [
        (i * band_count + j, (i ^ 24) * band_count + (j ^ 4)) for i in range(base_count) for j in range(band_count)
    ]

    def after(value, *others):
        return lax.optimization_barrier((value, *others))[0]

    jones, weights = lax.optimization_barrier((jones, tuple(weights[k] for k in range(4))))
    dual = jnp.zeros((rows, LANES), jnp.float32)
    residual = None
    for iteration in range(ITERS):
        if iteration:
            pieces = [jones] + along_x([jones] * 3)
            target = jones + dual / penalty
            pair = jnp.stack([target, lax.ppermute(target, both_axes, across_z)])
            pair = after(pair, *pieces[1:])
            four = [*pair, *base_swap(pair, 1)]
            meant = sum(weights[k][:, None, None] * four[k] for k in range(4))
        *terms, residual = iterate(core_scalar, pieces, sky, other_sky, seen, place, column)
        last_one = iteration + 1 == ITERS
        if last_one:
            terms, residual, meant = lax.optimization_barrier((terms, residual, meant))
        received = along_x(terms[1:])
        if iteration:
            came = band_swap(after(meant[1:3], terms[0]), 1)
            further = meant[3] + came[1]
            consensus = meant[0] + came[0] + band_swap(further, 3)
            dual = dual + penalty * (jones - consensus)
            jones_next = jones - step_size * (dual + penalty * (jones - consensus))
        else:
            jones_next = jones
        summed = terms[0] + received[0] + received[1] + received[2]
        if not last_one:
            others = along_z([summed] * 3)
            jones = jones_next + step_size * (summed + others[0] + others[1] + others[2])
    per_station = 2 * own_stations
    here, there = residual[:, :base_dev], base_swap(residual[:, base_dev:], 1)
    residual_out = jnp.where(core == 0, jnp.stack([here, there]), jnp.stack([there, here]))
    turned_sum = summed.T
    parts = [lax.dynamic_slice_in_dim(turned_sum, (z ^ k) * per_station, per_station, 0) for k in range(4)]
    others = along_z(parts[1:])
    residual_out, others = lax.optimization_barrier((residual_out, others))
    last = lax.dynamic_slice_in_dim(jones_next.T, z * per_station, per_station, 0)
    last = last + step_size * (parts[0] + others[0] + others[1] + others[2])
    last = last.reshape(2, own_stations, rows)
    kept, given = mine_of(last), base_swap(theirs_of(last), 1)
    both = jnp.where(core == 0, jnp.stack([kept, given]), jnp.stack([given, kept]))
    jones_out = both.reshape(sub_dev, own_stations, 8, dirs).transpose(0, 3, 2, 1)
    return (jones_out, residual_out)


def solution(mesh):
    return jax.shard_map(
        per_device,
        mesh=mesh,
        in_specs=(
            P("band", None, None, "base"),
            P("band", None, "base"),
            P("band", None, None, "base"),
            P("base"),
            P("base"),
        ),
        out_specs=(P("band", None, None, "base"), P("band", None, "base")),
        check_vma=False,
    )
```
